128 devices in a mesh: pipe: 2 (over y_hi), vocab: 8 (over x, core), dp: 8 (over z, y_lo).
Axes of the slice: x: 4, y: 4 (y_hi: 2, y_lo: 2; y = y_hi * 2 + y_lo), z: 4, core: 2. Of those that a mesh axis runs over, the one named last changes fastest.
Arguments:
- hidden: bfloat16 [2048, 7168], P(('pipe', 'dp')), may hold values from -750 to 750
- gain: bfloat16 [7168], replicated, may hold values from 0.5 to 1.5
- targets: int32 [2048], P(('pipe', 'dp')), may hold values from 0 to 32767
- table: bfloat16 [32768, 7168], P(('vocab', 'dp')), may hold values from -8 to 8
Outputs:
- hidden_grad: bfloat16 [2048, 7168], P(('pipe', 'dp'))
- table_grad: bfloat16 [32768, 7168], P(('vocab', 'dp'), 'pipe')
- token_loss: float32 [2048], P(('pipe', 'dp'))
The draws below stay inside these ranges and needn't reach their ends.
All inputs are finite; a program needn't handle non-finite values.
Results may differ from the reference program's by a relative error of at most 0.022.
Values may be sent and summed in bfloat16 or wider, within the bound.
No kernel may reach another device: no remote copies, remote signals or barrier semaphores. Data moves between devices by JAX's collectives and lax.ppermute only.
A program may use at most 128 MiB of HBM per device.

```python
import math
import jax
import jax.numpy as jnp
import numpy as np
from jax import lax

D = 7168
VOC_DEV = 512
GROUP = 1024
TOKENS = 2048
SHARDS = 64
VOCAB = 32768
N_PIPE = 2


def draw_hidden(key, part):
    key = jax.random.fold_in(key, 5)
    subkeys = jax.random.split(key, 3)
    col_scale = jnp.exp(jax.random.uniform(subkeys[0], (D,)) * math.log(10.0))
    row_scale = jnp.exp(jax.random.uniform(subkeys[1], (TOKENS, 1)) * math.log(10.0))
    values = jnp.clip(jax.random.normal(subkeys[2], (TOKENS, D)), -6.0, 6.0) * col_scale * row_scale
    return values.astype(jnp.bfloat16)


def draw_table(key, part):
    key = jax.random.fold_in(key, 9)
    spread = 3.0 / math.sqrt(D)
    values = jnp.clip(jax.random.normal(key, (VOCAB, D)), -6.0, 6.0) * spread
    return values.astype(jnp.bfloat16)


def with_ends(drawn, own_key, low, high):
    dims = drawn.shape
    index_at = [jax.random.randint(jax.random.fold_in(own_key, axis), (), 0, dims[axis]) for axis in range(len(dims))]
    drawn = drawn.at[tuple(index_at)].set(low)
    longest = dims.index(max(dims))
    index_at[longest] = (index_at[longest] + 1) % dims[longest]
    return drawn.at[tuple(index_at)].set(high)


def rank_table(count, skew):
    weights = [(1 << 20) // math.isqrt(rank ** skew) + 1 for rank in range(1, count + 1)]
    width = 1 + sum(weights) // (1 << 30)
    return np.cumsum(np.array([max(1, weight // width) for weight in weights]))


def ranked(key, extent, count, lean):
    listing = rank_table(count, lean)
    ticket = jax.random.randint(jax.random.fold_in(key, 1), extent, 0, int(listing[count - 1]))
    rank = jnp.searchsorted(jnp.asarray(listing, jnp.int32), ticket, side="right")
    return jax.random.permutation(jax.random.fold_in(key, 2), count)[rank].astype(jnp.int32)


def setup_inputs(seed: int = 0) -> dict:
    key_of = jax.random.split(jax.random.key(seed), 5)
    hidden = draw_hidden(jax.random.fold_in(key_of[4], 71), 0)
    gain = jnp.clip(1.0 + 0.1 * jax.random.normal(key_of[1], (D,), jnp.float32), 0.5, 1.5).astype(jnp.bfloat16)
    targets = with_ends(ranked(key_of[2], (TOKENS,), VOCAB, 2), jax.random.fold_in(key_of[2], 3), 0, VOCAB - 1).astype(jnp.int32)
    table = draw_table(jax.random.fold_in(key_of[4], 71), 0)
    return {"hidden": hidden, "gain": gain, "targets": targets, "table": table}


NORM_EPS = 1e-06

def reference(hidden, gain, targets, table):
    hidden_wide = hidden.astype(jnp.float32)
    inverse = lax.rsqrt(lax.optimization_barrier(jnp.mean(hidden_wide * hidden_wide, axis=1, keepdims=True)) + NORM_EPS)
    gain_wide = gain.astype(jnp.float32)
    normed = (hidden_wide * inverse * gain_wide).astype(jnp.bfloat16)
    shard_table = table.reshape(SHARDS, VOC_DEV, D)
    columns = jnp.arange(VOCAB, dtype=jnp.int32)
    losses = []
    grads = []
    table_total = jnp.zeros((VOCAB, D), jnp.float32)
    for pipe_end in range(N_PIPE):
        end_rows = normed[pipe_end * GROUP:(pipe_end + 1) * GROUP]
        wanted = targets[pipe_end * GROUP:(pipe_end + 1) * GROUP]
        logits = jnp.dot(end_rows, table.T, preferred_element_type=jnp.float32)
        row_top = lax.optimization_barrier(jnp.max(logits, axis=1, keepdims=True))
        row_total = lax.optimization_barrier(jnp.sum(jnp.exp(logits - row_top), axis=1, keepdims=True))
        log_norm = row_top + jnp.log(row_total)
        is_target = columns[None, :] == wanted[:, None]
        picked = lax.optimization_barrier(jnp.sum(jnp.where(is_target, logits, jnp.zeros_like(logits)), axis=1))
        losses.append(log_norm[:, 0] - picked)
        dlogits = (jnp.exp(logits - log_norm) - is_target.astype(jnp.float32)).astype(jnp.bfloat16)
        end_grad = jnp.dot(dlogits.T, end_rows, preferred_element_type=jnp.float32)
        rounded = lax.optimization_barrier(end_grad.astype(jnp.bfloat16))
        table_total = table_total + rounded.astype(jnp.float32)

        def add_term(carry, inputs):
            shard_index, shard_rows = inputs
            grad_block = lax.dynamic_slice_in_dim(dlogits, (shard_index * VOC_DEV).astype(jnp.int32), VOC_DEV, 1)
            shard_term = jnp.dot(grad_block, shard_rows, preferred_element_type=jnp.float32)
            shard_term = lax.optimization_barrier(shard_term.astype(jnp.bfloat16))
            return (carry + shard_term.astype(jnp.float32), None)
        normed_grad, _ = lax.scan(add_term, jnp.zeros((GROUP, D), jnp.float32), (jnp.arange(SHARDS, dtype=jnp.int32), shard_table))
        grads.append(normed_grad)
    normed_grad = jnp.concatenate(grads, axis=0)
    upward = normed_grad * gain_wide
    inner_sum = lax.optimization_barrier(jnp.sum(upward * hidden_wide, axis=1, keepdims=True))
    hidden_grad = (inverse * upward - hidden_wide * (inverse * inverse * inverse) * inner_sum / D).astype(jnp.bfloat16)
    return (hidden_grad, table_total.astype(jnp.bfloat16), jnp.concatenate(losses, axis=0))
```

```python
import jax
import jax.numpy as jnp
from jax import lax
from jax.sharding import PartitionSpec as P

NORM_EPS = 1e-06


def norm_backward(normed_grad, hidden_wide, inverse, gain_wide):
    upward = normed_grad * gain_wide
    inner_sum = jnp.sum(upward * hidden_wide, axis=1, keepdims=True)
    result = (
        inverse * upward
        - hidden_wide * (inverse * inverse * inverse) * inner_sum / hidden_wide.shape[1]
    )
    return result.astype(jnp.bfloat16)


def on_device(hidden, gain, targets, table):
    tok_rows, width = hidden.shape
    vocab_rows = table.shape[0]
    n_vocab, n_dp, n_pipe = lax.axis_size("vocab"), lax.axis_size("dp"), lax.axis_size("pipe")
    my_vocab, my_dp, my_pipe = lax.axis_index("vocab"), lax.axis_index("dp"), lax.axis_index("pipe")
    part = tok_rows // n_vocab

    hidden_wide = hidden.astype(jnp.float32)
    inverse = lax.rsqrt(jnp.mean(hidden_wide * hidden_wide, axis=1, keepdims=True) + NORM_EPS)
    gain_wide = gain.astype(jnp.float32)
    normed = (hidden_wide * inverse * gain_wide).astype(jnp.bfloat16)

    mine = lax.dynamic_slice_in_dim(normed, my_vocab * part, part)
    over_dp = lax.all_gather(mine, "dp", axis=0, tiled=True)
    gathered = lax.all_gather(over_dp, "vocab", axis=0, tiled=True)
    spread = jnp.broadcast_to(targets.reshape(1, 1, tok_rows), (n_dp, 1, tok_rows))
    wanted = lax.all_to_all(spread, "dp", 0, 0)
    wanted = wanted.reshape(n_dp, n_vocab, part).transpose(1, 0, 2).reshape(-1)

    logits = lax.dot_general(
        gathered, table, (((1,), (1,)), ((), ())), preferred_element_type=jnp.float32
    )
    first_row = (my_vocab * n_dp + my_dp) * vocab_rows
    columns = lax.broadcasted_iota(jnp.int32, (1, vocab_rows), 1) + first_row
    is_target = columns == wanted[:, None]
    picked = jnp.sum(jnp.where(is_target, logits, jnp.zeros_like(logits)), axis=1)
    local_top = jnp.max(logits, axis=1)
    local_total = jnp.sum(jnp.exp(logits - local_top[:, None]), axis=1)

    group = ("vocab", "dp")
    n_group = n_vocab * n_dp
    stats = jnp.stack(
        [s.reshape(n_group, part) for s in (local_top, local_total, picked)], axis=1
    )
    stats = lax.all_to_all(stats, group, 0, 0, tiled=True)
    tops, totals, picks = stats[:, 0], stats[:, 1], stats[:, 2]
    row_top = jnp.max(tops, axis=0)
    row_total = jnp.sum(totals * jnp.exp(tops - row_top), axis=0)
    own_norm = row_top + jnp.log(row_total)
    own_loss = own_norm - jnp.sum(picks, axis=0)
    both = jnp.stack([own_norm, own_loss])
    both = lax.all_to_all(
        jnp.broadcast_to(both[None], (n_group, 2, part)), group, 0, 0, tiled=True
    )
    log_norm = both[:, 0].reshape(-1)
    loss = both[:, 1].reshape(n_vocab, n_dp, part)
    token_loss = lax.dynamic_slice_in_dim(loss, my_dp, 1, axis=1).reshape(-1)

    dlogits = (jnp.exp(logits - log_norm[:, None]) - is_target.astype(jnp.float32)).astype(
        jnp.bfloat16
    )
    half = width // n_pipe

    def table_half(end):
        cols = lax.dynamic_slice_in_dim(gathered, end * half, half, axis=1)
        return lax.dot_general(
            dlogits, cols, (((0,), (0,)), ((), ())), preferred_element_type=jnp.float32
        )

    sent = table_half((my_pipe + 1) % n_pipe).astype(jnp.bfloat16)
    received = lax.ppermute(sent, "pipe", [(i, (i + 1) % n_pipe) for i in range(n_pipe)])

    replica_sum = jnp.dot(dlogits, table, preferred_element_type=jnp.float32).astype(jnp.bfloat16)
    over_vocab = lax.psum_scatter(replica_sum, "vocab", scatter_dimension=0, tiled=True)
    summed = lax.psum_scatter(over_vocab, "dp", scatter_dimension=0, tiled=True)
    table_grad = (table_half(my_pipe) + received.astype(jnp.float32)).astype(jnp.bfloat16)
    normed_grad = lax.all_gather(summed, "vocab", axis=0, tiled=True).astype(jnp.float32)
    hidden_grad = norm_backward(normed_grad, hidden_wide, inverse, gain_wide)
    return (hidden_grad, table_grad, token_loss)


def solution(mesh):
    placed = (P(("pipe", "dp"), None), P(), P(("pipe", "dp")), P(("vocab", "dp"), None))
    return jax.shard_map(
        on_device,
        mesh=mesh,
        in_specs=placed,
        out_specs=(P(("pipe", "dp"), None), P(("vocab", "dp"), "pipe"), P(("pipe", "dp"))),
        check_vma=False,
    )
```

```python
import jax
import jax.numpy as jnp
from jax import lax
from jax.sharding import PartitionSpec as P

NORM_EPS = 1e-06
NX, NC, NZ, NY = 4, 2, 4, 2


def hop(array, dx=0, dc=0, dz=0, dy=0):
    pairs = []
    for x in range(NX):
        for c in range(NC):
            for z in range(NZ):
                for y in range(NY):
                    here = ((x * NC + c) * NZ + z) * NY + y
                    there = (
                        ((x + dx) % NX * NC + (c + dc) % NC) * NZ + (z + dz) % NZ
                    ) * NY + (y + dy) % NY
                    pairs.append((here, there))
    return lax.ppermute(array, ("vocab", "dp"), pairs)


def put(buffer, block, *lead):
    block = block.reshape((1,) * len(lead) + buffer.shape[len(lead):])
    start = tuple(lead) + (0,) * (buffer.ndim - len(lead))
    return lax.dynamic_update_slice(buffer, block, start)


def take(buffer, *lead):
    start = tuple(lead) + (0,) * (buffer.ndim - len(lead))
    sizes = (1,) * len(lead) + buffer.shape[len(lead):]
    return lax.dynamic_slice(buffer, start, sizes).reshape(buffer.shape[len(lead):])


def dot(a, b, contract, out=jnp.float32):
    return lax.dot_general(
        a, b, (contract, ((), ())), preferred_element_type=jnp.float32
    ).astype(out)


def on_device(hidden, gain, targets, table):
    tok_rows, width = hidden.shape
    vocab_rows = table.shape[0]
    half = width // 2
    bf16, f32 = jnp.bfloat16, jnp.float32
    vocab, dp, pipe = lax.axis_index("vocab"), lax.axis_index("dp"), lax.axis_index("pipe")
    x, c = vocab // NC, vocab % NC
    z, y = dp // NY, dp % NY
    group = NX * NC * NZ * NY
    part = tok_rows // (NX * NC)
    side = tok_rows // NC
    far = side * NZ * NY
    first = c * side + x * part
    own_col, other_col = pipe * half, (1 - pipe) * half

    gain_wide = gain.astype(f32)

    def scale(rows):
        wide = rows.astype(f32)
        inverse = lax.rsqrt(jnp.mean(wide * wide, axis=1, keepdims=True) + NORM_EPS)
        return wide, inverse, (wide * inverse * gain_wide).astype(bf16)

    hidden_mine, inverse_mine, normed_mine = scale(
        lax.dynamic_slice_in_dim(hidden, first, part)
    )
    mine1 = lax.dynamic_slice(normed_mine, (0, own_col), (part, half))
    seed = jnp.broadcast_to(mine1[None], (NZ * NY, part, half))
    near = lax.all_to_all(seed, "dp", 0, 0, tiled=True)
    _, _, normed_side = scale(lax.dynamic_slice_in_dim(hidden, c * side, side))
    mine2 = lax.dynamic_slice(normed_side, (0, other_col), (side, half))
    mine2, near, targets = lax.optimization_barrier((mine2, near, targets))
    rows1 = lax.all_gather(near.reshape(-1, half), "vocab", axis=0, tiled=True)

    partner = hop(mine2, dy=1)
    rows2 = jnp.zeros((NC, NY, NZ, side, half), bf16)
    for block, at in ((mine2, y), (partner, 1 - y)):
        gathered = put(jnp.zeros((NZ, side, half), bf16), block, z)
        for dz in (1, 3, 2):
            gathered = put(gathered, hop(block, dz=dz), (z - dz) % NZ)
        rows2 = put(rows2, gathered, c, at)
        rows2 = put(rows2, hop(gathered, dc=1), 1 - c, at)
    rows2 = rows2.reshape(-1, half)

    spread = jnp.broadcast_to(targets.reshape(1, tok_rows), (NZ * NY, tok_rows))
    wanted = lax.all_to_all(spread, "dp", 0, 0, tiled=True)
    wanted = wanted.reshape(NZ * NY, NC, NX, part).transpose(2, 1, 0, 3).reshape(-1)

    table1 = lax.dynamic_slice(table, (0, own_col), (vocab_rows, half))
    table2 = lax.dynamic_slice(table, (0, other_col), (vocab_rows, half))
    logits1 = dot(rows1, table1, ((1,), (1,)))
    logits2 = dot(rows2, table2, ((1,), (1,)))
    logits2 = logits2.reshape(NC, NY, NZ, NX, part, vocab_rows).transpose(3, 0, 2, 1, 4, 5)
    logits = logits1 + logits2.reshape(logits1.shape)

    first_row = (vocab * NZ * NY + dp) * vocab_rows
    columns = lax.broadcasted_iota(jnp.int32, (1, vocab_rows), 1) + first_row
    is_target = columns == wanted[:, None]
    picked = jnp.sum(jnp.where(is_target, logits, jnp.zeros_like(logits)), axis=1)
    local_top = jnp.max(logits, axis=1)
    local_norm = local_top + jnp.log(jnp.sum(jnp.exp(logits - local_top[:, None]), axis=1))
    picked = picked.reshape(NX * NC, NZ * NY, part).transpose(1, 0, 2).reshape(NZ * NY, tok_rows)
    stats = jnp.concatenate(
        [
            jnp.broadcast_to(local_norm[None], (group, local_norm.shape[0])),
            jnp.tile(picked, (NX * NC, 1)),
        ],
        axis=1,
    )
    stats = lax.all_to_all(stats, ("vocab", "dp"), 0, 0, tiled=True)
    norms, picks = stats[:, : local_norm.shape[0]], stats[:, local_norm.shape[0] :]
    row_top = jnp.max(norms, axis=0)
    log_norm = row_top + jnp.log(jnp.sum(jnp.exp(norms - row_top), axis=0))
    own_norm = lax.dynamic_slice_in_dim(
        log_norm.reshape(NX * NC, NZ * NY, part), dp, 1, axis=1
    ).reshape(-1)
    token_loss = (own_norm - jnp.sum(picks, axis=0)).reshape(NX, NC, part)
    token_loss = token_loss.transpose(1, 0, 2).reshape(-1)

    grad_a = (jnp.exp(logits - log_norm[:, None]) - is_target.astype(f32)).astype(bf16)
    grad_b = grad_a.reshape(NX, NC, NZ, NY, part, vocab_rows).transpose(1, 3, 2, 0, 4, 5)
    grad_b = grad_b.reshape(NC, far, vocab_rows)

    swap = [(0, 1), (1, 0)]
    early = vocab_rows * 3 // 4
    all_b = grad_b.reshape(-1, vocab_rows)
    sent_grad = dot(all_b[:, :early], rows2, ((0,), (0,)), bf16)
    late_grad = dot(all_b[:, early:], rows2, ((0,), (0,)), bf16)
    sent_grad, late_grad, grad_a, grad_b = lax.optimization_barrier(
        (sent_grad, late_grad, grad_a, grad_b)
    )
    received = lax.ppermute(sent_grad, "pipe", swap)
    sent = dot(take(grad_b, 1 - c), table2, ((1,), (0,)), bf16)
    sent, grad_a = lax.optimization_barrier((sent, grad_a))
    sent = hop(sent, dc=1)
    sums1 = dot(grad_a, table1, ((1,), (0,)), bf16)
    sums1, grad_b = lax.optimization_barrier((sums1, grad_b))
    over_vocab = lax.psum_scatter(sums1, "vocab", scatter_dimension=0, tiled=True)
    sums2 = (dot(take(grad_b, c), table2, ((1,), (0,))) + sent.astype(f32)).astype(bf16)
    sums2 = sums2.reshape(NY, NZ, side, half)
    z_blocks = [
        lax.dynamic_slice_in_dim(sums2, (z + dz) % NZ, 1, axis=1).reshape(NY, NX, part, half)
        for dz in range(NZ)
    ]
    *z_blocks, grad_a = lax.optimization_barrier((*z_blocks, grad_a))

    own_grad = dot(grad_a, rows1, ((0,), (0,)))

    total2 = z_blocks[0].astype(f32)
    for dz in (1, 3, 2):
        total2 = total2 + hop(z_blocks[dz], dz=dz).astype(f32)
    total2 = total2.astype(bf16)
    x_blocks = [
        lax.dynamic_slice_in_dim(total2, (x + dx) % NX, 1, axis=1).reshape(NY, part, half)
        for dx in range(NX)
    ]
    *x_blocks, own_grad = lax.optimization_barrier((*x_blocks, own_grad))
    mine2 = x_blocks[0].astype(f32)
    for dx in (1, 3, 2):
        mine2 = mine2 + hop(x_blocks[dx], dx=dx).astype(f32)
    mine2 = mine2.astype(bf16)
    mine2, over_vocab, received = lax.optimization_barrier((mine2, over_vocab, received))
    mine2 = take(mine2, y).astype(f32) + hop(take(mine2, 1 - y), dy=1).astype(f32)
    blocks = lax.all_to_all(over_vocab.reshape(-1, part, half), "dp", 0, 0, tiled=True)
    mine1 = jnp.sum(blocks.astype(f32), axis=0)
    mine1, mine2, late = lax.optimization_barrier((mine1, mine2, late_grad))
    late = lax.ppermute(late, "pipe", swap)

    own_first = pipe == 0
    normed_grad = jnp.concatenate(
        [jnp.where(own_first, mine1, mine2), jnp.where(own_first, mine2, mine1)], axis=1
    )
    upward = normed_grad * gain_wide
    inner_sum = jnp.sum(upward * hidden_mine, axis=1, keepdims=True)
    result = (
        inverse_mine * upward
        - hidden_mine * (inverse_mine * inverse_mine * inverse_mine) * inner_sum / width
    ).astype(bf16)
    along_x = put(jnp.zeros((NX, part, width), bf16), result, x)
    for dx in (1, 3, 2):
        along_x = put(along_x, hop(result, dx=dx), (x - dx) % NX)
    hidden_grad = put(jnp.zeros((NC, NX, part, width), bf16), along_x, c)
    hidden_grad = put(hidden_grad, hop(along_x, dc=1), 1 - c)
    received = jnp.concatenate([received, late], axis=0).astype(f32)
    table_grad = (own_grad + received).astype(bf16)
    return (hidden_grad.reshape(tok_rows, width), table_grad, token_loss)


def solution(mesh):
    placed = (P(("pipe", "dp"), None), P(), P(("pipe", "dp")), P(("vocab", "dp"), None))
    return jax.shard_map(
        on_device,
        mesh=mesh,
        in_specs=placed,
        out_specs=(P(("pipe", "dp"), None), P(("vocab", "dp"), "pipe"), P(("pipe", "dp"))),
        check_vma=False,
    )
```

```python
import jax
import jax.numpy as jnp
from jax import lax
from jax.experimental import pallas as pl
from jax.experimental.pallas import tpu as pltpu
from jax.sharding import PartitionSpec as P

NORM_EPS = 1e-06
NX, NC, NZ, NY = 4, 2, 4, 2
DIGIT = 256


def hop(array, dx=0, dc=0, dz=0, dy=0):
    pairs = []
    for x in range(NX):
        for c in range(NC):
            for z in range(NZ):
                for y in range(NY):
                    here = ((x * NC + c) * NZ + z) * NY + y
                    there = (
                        ((x + dx) % NX * NC + (c + dc) % NC) * NZ + (z + dz) % NZ
                    ) * NY + (y + dy) % NY
                    pairs.append((here, there))
    return lax.ppermute(array, ("vocab", "dp"), pairs)


def put(buffer, block, *lead):
    block = block.reshape((1,) * len(lead) + buffer.shape[len(lead):])
    start = tuple(lead) + (0,) * (buffer.ndim - len(lead))
    return lax.dynamic_update_slice(buffer, block, start)


def take(buffer, *lead):
    start = tuple(lead) + (0,) * (buffer.ndim - len(lead))
    sizes = (1,) * len(lead) + buffer.shape[len(lead):]
    return lax.dynamic_slice(buffer, start, sizes).reshape(buffer.shape[len(lead):])


def dot(a, b, contract, out=jnp.float32):
    return lax.dot_general(
        a, b, (contract, ((), ())), preferred_element_type=jnp.float32
    ).astype(out)


def backward_kernel(place, hidden, gain, mine1, mine2, far, result):
    part, width = hidden.shape
    own = mine1[...]
    other = mine2[...] + far[...].astype(jnp.float32)
    first = place[1] == 0
    grad = jnp.concatenate(
        [jnp.where(first, own, other), jnp.where(first, other, own)], axis=1
    )
    wide = hidden[...].astype(jnp.float32)
    inverse = lax.rsqrt(jnp.mean(wide * wide, axis=1, keepdims=True) + NORM_EPS)
    upward = grad * gain[...].astype(jnp.float32)
    inner_sum = jnp.sum(upward * wide, axis=1, keepdims=True)
    result[...] = (
        inverse * upward - wide * (inverse * inverse * inverse) * inner_sum / width
    ).astype(jnp.bfloat16)


def backward_call(place, hidden, gain, mine1, mine2, far, part):
    width = hidden.shape[1]
    whole = lambda a: pl.BlockSpec(a.shape, lambda i, p: (0, 0))
    return pl.pallas_call(
        backward_kernel,
        grid_spec=pltpu.PrefetchScalarGridSpec(
            num_scalar_prefetch=1,
            grid=(1,),
            in_specs=[
                pl.BlockSpec((part, width), lambda i, p: (p[0], 0)),
                pl.BlockSpec((1, width), lambda i, p: (0, 0)),
                whole(mine1), whole(mine2), whole(far),
            ],
            out_specs=pl.BlockSpec((part, width), lambda i, p: (0, 0)),
        ),
        out_shape=jax.ShapeDtypeStruct((part, width), jnp.bfloat16),
        compiler_params=pltpu.CompilerParams(vmem_limit_bytes=32 << 20),
        name="backward",
    )(place, hidden, gain.reshape(1, width), mine1, mine2, far)


def on_device(hidden, gain, targets, table):
    tok_rows, width = hidden.shape
    vocab_rows = table.shape[0]
    half = width // 2
    bf16, f32 = jnp.bfloat16, jnp.float32
    vocab, dp, pipe = lax.axis_index("vocab"), lax.axis_index("dp"), lax.axis_index("pipe")
    x, c = vocab // NC, vocab % NC
    z, y = dp // NY, dp % NY
    group = NX * NC * NZ * NY
    part = tok_rows // (NX * NC)
    side = tok_rows // NC
    far = side * NZ * NY
    first = c * side + x * part
    own_col, other_col = pipe * half, (1 - pipe) * half

    gain_wide = gain.astype(f32)
    place = jnp.stack([c * NX + x, pipe]).astype(jnp.int32)

    def scale(rows):
        wide = rows.astype(f32)
        inverse = lax.rsqrt(jnp.mean(wide * wide, axis=1, keepdims=True) + NORM_EPS)
        return (wide * inverse * gain_wide).astype(bf16)

    normed_mine = scale(lax.dynamic_slice_in_dim(hidden, first, part))
    mine1 = lax.dynamic_slice(normed_mine, (0, own_col), (part, half))
    digits = jnp.stack([targets // DIGIT, targets % DIGIT]).astype(bf16)
    digits = jnp.pad(digits, ((0, part - 2), (0, 0)))
    seed = jnp.concatenate([mine1, digits], axis=1)
    seed = jnp.broadcast_to(seed[None], (NZ * NY, part, half + tok_rows))
    near = lax.all_to_all(seed, "dp", 0, 0, tiled=True)
    normed_side = scale(lax.dynamic_slice_in_dim(hidden, c * side, side))
    mine2 = lax.dynamic_slice(normed_side, (0, other_col), (side, half))
    mine2, near = lax.optimization_barrier((mine2, near))
    rows1 = lax.all_gather(near[:, :, :half].reshape(-1, half), "vocab", axis=0, tiled=True)

    partner = hop(mine2, dy=1)
    rows2 = jnp.zeros((NC, NY, NZ, side, half), bf16)
    own_rows = put(jnp.zeros((NZ, side, half), bf16), mine2, z)
    far_rows = put(jnp.zeros((NZ, side, half), bf16), partner, z)
    near1, near3, near2 = (hop(mine2, dz=dz) for dz in (1, 3, 2))
    far2, far1, far3 = hop(partner, dz=2), hop(near1, dy=1), hop(near3, dy=1)
    near2, far1 = lax.optimization_barrier((near2, far1))
    for dz, near_block, far_block in ((1, near1, far1), (3, near3, far3), (2, near2, far2)):
        own_rows = put(own_rows, near_block, (z - dz) % NZ)
        far_rows = put(far_rows, far_block, (z - dz) % NZ)
    for block, at in ((own_rows, y), (far_rows, 1 - y)):
        rows2 = put(rows2, block, c, at)
        rows2 = put(rows2, hop(block, dc=1), 1 - c, at)
    rows2 = rows2.reshape(-1, half)

    wanted = near[:, :2, half:].astype(jnp.int32)
    wanted = wanted[:, 0] * DIGIT + wanted[:, 1]
    wanted = wanted.reshape(NZ * NY, NC, NX, part).transpose(2, 1, 0, 3).reshape(-1)

    table1 = lax.dynamic_slice(table, (0, own_col), (vocab_rows, half))
    table2 = lax.dynamic_slice(table, (0, other_col), (vocab_rows, half))
    table1, table2, wanted = lax.optimization_barrier((table1, table2, wanted))
    logits1 = dot(rows1, table1, ((1,), (1,)))
    logits2 = dot(rows2, table2, ((1,), (1,)))
    logits2 = logits2.reshape(NC, NY, NZ, NX, part, vocab_rows).transpose(3, 0, 2, 1, 4, 5)
    logits2 = logits2.reshape(logits1.shape)
    logits1, logits2 = lax.optimization_barrier((logits1, logits2))
    logits = logits1 + logits2

    first_row = (vocab * NZ * NY + dp) * vocab_rows
    columns = lax.broadcasted_iota(jnp.int32, (1, vocab_rows), 1) + first_row
    is_target = columns == wanted[:, None]
    picked = jnp.sum(jnp.where(is_target, logits, jnp.zeros_like(logits)), axis=1)
    local_top = jnp.max(logits, axis=1)
    local_norm = local_top + jnp.log(jnp.sum(jnp.exp(logits - local_top[:, None]), axis=1))
    picked = picked.reshape(NX * NC, NZ * NY, part).transpose(1, 0, 2).reshape(NZ * NY, tok_rows)
    stats = jnp.concatenate(
        [
            jnp.broadcast_to(local_norm[None], (group, local_norm.shape[0])),
            jnp.tile(picked, (NX * NC, 1)),
        ],
        axis=1,
    )
    stats = lax.all_to_all(stats, ("vocab", "dp"), 0, 0, tiled=True)
    norms, picks = stats[:, : local_norm.shape[0]], stats[:, local_norm.shape[0] :]
    row_top = jnp.max(norms, axis=0)
    log_norm = row_top + jnp.log(jnp.sum(jnp.exp(norms - row_top), axis=0))
    own_norm = lax.dynamic_slice_in_dim(
        log_norm.reshape(NX * NC, NZ * NY, part), dp, 1, axis=1
    ).reshape(-1)
    token_loss = (own_norm - jnp.sum(picks, axis=0)).reshape(NX, NC, part)
    token_loss = token_loss.transpose(1, 0, 2).reshape(-1)

    grad_a = (jnp.exp(logits - log_norm[:, None]) - is_target.astype(f32)).astype(bf16)
    grad_b = grad_a.reshape(NX, NC, NZ, NY, part, vocab_rows).transpose(1, 3, 2, 0, 4, 5)
    grad_b = grad_b.reshape(NC, far, vocab_rows)

    sums1 = dot(grad_a, table1, ((1,), (0,)), bf16)
    sums1, grad_a, grad_b = lax.optimization_barrier((sums1, grad_a, grad_b))
    over_vocab = lax.psum_scatter(sums1, "vocab", scatter_dimension=0, tiled=True)
    sent = dot(take(grad_b, 1 - c), table2, ((1,), (0,)), bf16)
    sent, grad_b = lax.optimization_barrier((sent, grad_b))
    sent = hop(sent, dc=1)

    swap = [(0, 1), (1, 0)]
    early = vocab_rows * 3 // 4
    all_b = grad_b.reshape(-1, vocab_rows)
    sent_grad = dot(all_b[:, :early], rows2, ((0,), (0,)), bf16)
    sent_grad, grad_b = lax.optimization_barrier((sent_grad, grad_b))
    received = lax.ppermute(sent_grad, "pipe", swap)

    sums2 = (dot(take(grad_b, c), table2, ((1,), (0,))) + sent.astype(f32)).astype(bf16)
    sums2 = sums2.reshape(NY, NZ, side, half)
    z_blocks = [
        lax.dynamic_slice_in_dim(sums2, (z + dz) % NZ, 1, axis=1).reshape(NY, NX, part, half)
        for dz in range(NZ)
    ]
    *z_blocks, grad_a, grad_b = lax.optimization_barrier((*z_blocks, grad_a, grad_b))
    late_grad = dot(grad_b.reshape(-1, vocab_rows)[:, early:], rows2, ((0,), (0,)), bf16)
    own_grad = dot(grad_a, rows1, ((0,), (0,)), bf16)

    total2 = z_blocks[0].astype(f32)
    for dz in (1, 3, 2):
        total2 = total2 + hop(z_blocks[dz], dz=dz).astype(f32)
    total2 = total2.astype(bf16)
    x_blocks = [
        lax.dynamic_slice_in_dim(total2, (x + dx) % NX, 1, axis=1).reshape(NY, part, half)
        for dx in range(NX)
    ]
    *x_blocks, own_grad, late_grad, over_vocab = lax.optimization_barrier(
        (*x_blocks, own_grad, late_grad, over_vocab)
    )
    mine2 = x_blocks[0].astype(f32)
    for dx in (1, 3, 2):
        mine2 = mine2 + hop(x_blocks[dx], dx=dx).astype(f32)
    mine2 = mine2.astype(bf16)
    blocks = lax.all_to_all(over_vocab.reshape(-1, part, half), "dp", 0, 0, tiled=True)
    mine1 = jnp.sum(blocks.astype(f32), axis=0)
    mine1, mine2, received = lax.optimization_barrier((mine1, mine2, received))
    far = hop(take(mine2, 1 - y), dy=1)
    mine2 = take(mine2, y).astype(f32)
    far, late, received = lax.optimization_barrier((far, late_grad, received))
    late = lax.ppermute(late, "pipe", swap)

    result = backward_call(place, hidden, gain, mine1, mine2, far, part)
    along_x = put(jnp.zeros((NX, part, width), bf16), result, x)
    for dx in (1, 3, 2):
        along_x = put(along_x, hop(result, dx=dx), (x - dx) % NX)
    hidden_grad = put(jnp.zeros((NC, NX, part, width), bf16), along_x, c)
    hidden_grad = put(hidden_grad, hop(along_x, dc=1), 1 - c)
    own_wide = own_grad.astype(f32)
    table_grad = lax.dynamic_update_slice(
        jnp.zeros((vocab_rows, half), bf16),
        (own_wide[:early] + received.astype(f32)).astype(bf16),
        (0, 0),
    )
    table_grad = lax.dynamic_update_slice(
        table_grad, (own_wide[early:] + late.astype(f32)).astype(bf16), (early, 0)
    )
    return (hidden_grad.reshape(tok_rows, width), table_grad, token_loss)


def solution(mesh):
    placed = (P(("pipe", "dp"), None), P(), P(("pipe", "dp")), P(("vocab", "dp"), None))
    return jax.shard_map(
        on_device,
        mesh=mesh,
        in_specs=placed,
        out_specs=(P(("pipe", "dp"), None), P(("vocab", "dp"), "pipe"), P(("pipe", "dp"))),
        check_vma=False,
    )
```

```python
import jax
import jax.numpy as jnp
from jax import lax
from jax.experimental import pallas as pl
from jax.experimental.pallas import tpu as pltpu
from jax.sharding import PartitionSpec as P

NORM_EPS = 1e-06
NX, NC, NZ, NY = 4, 2, 4, 2
DIGIT = 256


def hop(array, dx=0, dc=0, dz=0, dy=0):
    pairs = []
    for x in range(NX):
        for c in range(NC):
            for z in range(NZ):
                for y in range(NY):
                    here = ((x * NC + c) * NZ + z) * NY + y
                    there = (
                        ((x + dx) % NX * NC + (c + dc) % NC) * NZ + (z + dz) % NZ
                    ) * NY + (y + dy) % NY
                    pairs.append((here, there))
    return lax.ppermute(array, ("vocab", "dp"), pairs)


def put(buffer, block, *lead):
    block = block.reshape((1,) * len(lead) + buffer.shape[len(lead):])
    start = tuple(lead) + (0,) * (buffer.ndim - len(lead))
    return lax.dynamic_update_slice(buffer, block, start)


def take(buffer, *lead):
    start = tuple(lead) + (0,) * (buffer.ndim - len(lead))
    sizes = (1,) * len(lead) + buffer.shape[len(lead):]
    return lax.dynamic_slice(buffer, start, sizes).reshape(buffer.shape[len(lead):])


def dot(a, b, contract, out=jnp.float32):
    return lax.dot_general(
        a, b, (contract, ((), ())), preferred_element_type=jnp.float32
    ).astype(out)


def backward_kernel(place, hidden, gain, mine1, mine2, far, result):
    part, width = hidden.shape
    own = mine1[...]
    other = mine2[...] + far[...].astype(jnp.float32)
    first = place[1] == 0
    grad = jnp.concatenate(
        [jnp.where(first, own, other), jnp.where(first, other, own)], axis=1
    )
    wide = hidden[...].astype(jnp.float32)
    inverse = lax.rsqrt(jnp.mean(wide * wide, axis=1, keepdims=True) + NORM_EPS)
    upward = grad * gain[...].astype(jnp.float32)
    inner_sum = jnp.sum(upward * wide, axis=1, keepdims=True)
    result[...] = (
        inverse * upward - wide * (inverse * inverse * inverse) * inner_sum / width
    ).astype(jnp.bfloat16)


def backward_call(place, hidden, gain, mine1, mine2, far, part):
    width = hidden.shape[1]
    whole = lambda a: pl.BlockSpec(a.shape, lambda i, p: (0, 0))
    return pl.pallas_call(
        backward_kernel,
        grid_spec=pltpu.PrefetchScalarGridSpec(
            num_scalar_prefetch=1,
            grid=(1,),
            in_specs=[
                pl.BlockSpec((part, width), lambda i, p: (p[0], 0)),
                pl.BlockSpec((1, width), lambda i, p: (0, 0)),
                whole(mine1), whole(mine2), whole(far),
            ],
            out_specs=pl.BlockSpec((part, width), lambda i, p: (0, 0)),
        ),
        out_shape=jax.ShapeDtypeStruct((part, width), jnp.bfloat16),
        compiler_params=pltpu.CompilerParams(vmem_limit_bytes=32 << 20),
        name="backward",
    )(place, hidden, gain.reshape(1, width), mine1, mine2, far)


def on_device(hidden, gain, targets, table):
    tok_rows, width = hidden.shape
    vocab_rows = table.shape[0]
    half = width // 2
    bf16, f32 = jnp.bfloat16, jnp.float32
    vocab, dp, pipe = lax.axis_index("vocab"), lax.axis_index("dp"), lax.axis_index("pipe")
    x, c = vocab // NC, vocab % NC
    z, y = dp // NY, dp % NY
    group = NX * NC * NZ * NY
    part = tok_rows // (NX * NC)
    side = tok_rows // NC
    far = side * NZ * NY
    first = c * side + x * part
    own_col, other_col = pipe * half, (1 - pipe) * half

    gain_wide = gain.astype(f32)
    place = jnp.stack([c * NX + x, pipe]).astype(jnp.int32)

    def scale(rows):
        wide = rows.astype(f32)
        inverse = lax.rsqrt(jnp.mean(wide * wide, axis=1, keepdims=True) + NORM_EPS)
        return (wide * inverse * gain_wide).astype(bf16)

    normed_mine = scale(lax.dynamic_slice_in_dim(hidden, first, part))
    mine1 = lax.dynamic_slice(normed_mine, (0, own_col), (part, half))
    digits = jnp.stack([targets // DIGIT, targets % DIGIT]).astype(bf16)
    digits = jnp.pad(digits, ((0, part - 2), (0, 0)))
    seed = jnp.concatenate([mine1, digits], axis=1)
    seed = jnp.broadcast_to(seed[None], (NZ * NY, part, half + tok_rows))
    near = lax.all_to_all(seed, "dp", 0, 0, tiled=True)
    normed_side = scale(lax.dynamic_slice_in_dim(hidden, c * side, side))
    mine2 = lax.dynamic_slice(normed_side, (0, other_col), (side, half))
    mine2, near = lax.optimization_barrier((mine2, near))
    rows1 = lax.all_gather(near[:, :, :half].reshape(-1, half), "vocab", axis=0, tiled=True)

    partner = hop(mine2, dy=1)
    rows2 = jnp.zeros((NC, NY, NZ, side, half), bf16)
    own_rows = put(jnp.zeros((NZ, side, half), bf16), mine2, z)
    far_rows = put(jnp.zeros((NZ, side, half), bf16), partner, z)
    near1, near3, near2 = (hop(mine2, dz=dz) for dz in (1, 3, 2))
    far2, far1, far3 = hop(partner, dz=2), hop(near1, dy=1), hop(near3, dy=1)
    near2, far1 = lax.optimization_barrier((near2, far1))
    for dz, near_block, far_block in ((1, near1, far1), (3, near3, far3), (2, near2, far2)):
        own_rows = put(own_rows, near_block, (z - dz) % NZ)
        far_rows = put(far_rows, far_block, (z - dz) % NZ)
    for block, at in ((own_rows, y), (far_rows, 1 - y)):
        rows2 = put(rows2, block, c, at)
        rows2 = put(rows2, hop(block, dc=1), 1 - c, at)
    rows2 = rows2.reshape(-1, half)

    wanted = near[:, :2, half:].astype(jnp.int32)
    wanted = wanted[:, 0] * DIGIT + wanted[:, 1]
    wanted = wanted.reshape(NZ * NY, NC, NX, part).transpose(2, 1, 0, 3).reshape(-1)

    table1 = lax.dynamic_slice(table, (0, own_col), (vocab_rows, half))
    table2 = lax.dynamic_slice(table, (0, other_col), (vocab_rows, half))
    table1, table2, wanted = lax.optimization_barrier((table1, table2, wanted))
    logits1 = dot(rows1, table1, ((1,), (1,)))
    logits2 = dot(rows2, table2, ((1,), (1,)))
    logits2 = logits2.reshape(NC, NY, NZ, NX, part, vocab_rows).transpose(3, 0, 2, 1, 4, 5)
    logits2 = logits2.reshape(logits1.shape)
    logits1, logits2 = lax.optimization_barrier((logits1, logits2))
    logits = logits1 + logits2

    first_row = (vocab * NZ * NY + dp) * vocab_rows
    columns = lax.broadcasted_iota(jnp.int32, (1, vocab_rows), 1) + first_row
    is_target = columns == wanted[:, None]
    picked = jnp.sum(jnp.where(is_target, logits, jnp.zeros_like(logits)), axis=1)
    local_top = jnp.max(logits, axis=1)
    local_norm = local_top + jnp.log(jnp.sum(jnp.exp(logits - local_top[:, None]), axis=1))
    picked = picked.reshape(NX * NC, NZ * NY, part).transpose(1, 0, 2).reshape(NZ * NY, tok_rows)
    stats = jnp.concatenate(
        [
            jnp.broadcast_to(local_norm[None], (group, local_norm.shape[0])),
            jnp.tile(picked, (NX * NC, 1)),
        ],
        axis=1,
    )
    stats = lax.all_to_all(stats, ("vocab", "dp"), 0, 0, tiled=True)
    norms, picks = stats[:, : local_norm.shape[0]], stats[:, local_norm.shape[0] :]
    row_top = jnp.max(norms, axis=0)
    log_norm = row_top + jnp.log(jnp.sum(jnp.exp(norms - row_top), axis=0))
    own_norm = lax.dynamic_slice_in_dim(
        log_norm.reshape(NX * NC, NZ * NY, part), dp, 1, axis=1
    ).reshape(-1)
    token_loss = (own_norm - jnp.sum(picks, axis=0)).reshape(NX, NC, part)
    token_loss = token_loss.transpose(1, 0, 2).reshape(-1)

    grad_a = (jnp.exp(logits - log_norm[:, None]) - is_target.astype(f32)).astype(bf16)
    grad_b = grad_a.reshape(NX, NC, NZ, NY, part, vocab_rows).transpose(1, 3, 2, 0, 4, 5)
    grad_b = grad_b.reshape(NC, far, vocab_rows)

    sums1 = dot(grad_a, table1, ((1,), (0,)), bf16)
    sums1, grad_a, grad_b = lax.optimization_barrier((sums1, grad_a, grad_b))
    over_vocab = lax.psum_scatter(sums1, "vocab", scatter_dimension=0, tiled=True)
    sent = dot(take(grad_b, 1 - c), table2, ((1,), (0,)), bf16)
    start, early = half // 14, half * 6 // 7
    first_grad = dot(grad_b.reshape(-1, vocab_rows), rows2[:, :start], ((0,), (0,)), bf16)
    sent, first_grad, grad_b = lax.optimization_barrier((sent, first_grad, grad_b))
    swap = [(0, 1), (1, 0)]
    first_grad = lax.ppermute(first_grad, "pipe", swap)
    sent = hop(sent, dc=1)

    all_b = grad_b.reshape(-1, vocab_rows)
    sent_grad = dot(all_b, rows2[:, start:early], ((0,), (0,)), bf16)
    sent_grad, grad_b = lax.optimization_barrier((sent_grad, grad_b))
    received = lax.ppermute(sent_grad, "pipe", swap)
    first_grad, grad_b = lax.optimization_barrier((first_grad, grad_b))

    sums2 = (dot(take(grad_b, c), table2, ((1,), (0,))) + sent.astype(f32)).astype(bf16)
    sums2 = sums2.reshape(NY, NZ, side, half)
    z_blocks = [
        lax.dynamic_slice_in_dim(sums2, (z + dz) % NZ, 1, axis=1).reshape(NY, NX, part, half)
        for dz in range(NZ)
    ]
    *z_blocks, grad_a, grad_b = lax.optimization_barrier((*z_blocks, grad_a, grad_b))
    late_grad = dot(grad_b.reshape(-1, vocab_rows), rows2[:, early:], ((0,), (0,)), bf16)
    own_grad = dot(grad_a, rows1, ((0,), (0,)), bf16)

    total2 = z_blocks[0].astype(f32)
    for dz in (1, 3, 2):
        total2 = total2 + hop(z_blocks[dz], dz=dz).astype(f32)
    total2 = total2.astype(bf16)
    x_blocks = [
        lax.dynamic_slice_in_dim(total2, (x + dx) % NX, 1, axis=1).reshape(NY, part, half)
        for dx in range(NX)
    ]
    *x_blocks, own_grad, late_grad, over_vocab = lax.optimization_barrier(
        (*x_blocks, own_grad, late_grad, over_vocab)
    )
    mine2 = x_blocks[0].astype(f32)
    for dx in (1, 3, 2):
        mine2 = mine2 + hop(x_blocks[dx], dx=dx).astype(f32)
    mine2 = mine2.astype(bf16)
    blocks = lax.all_to_all(over_vocab.reshape(-1, part, half), "dp", 0, 0, tiled=True)
    mine1 = jnp.sum(blocks.astype(f32), axis=0)
    mine1, mine2, received = lax.optimization_barrier((mine1, mine2, received))
    far = hop(take(mine2, 1 - y), dy=1)
    mine2 = take(mine2, y).astype(f32)
    far, late, received = lax.optimization_barrier((far, late_grad, received))
    late = lax.ppermute(late, "pipe", swap)

    result = backward_call(place, hidden, gain, mine1, mine2, far, part)
    along_x = put(jnp.zeros((NX, part, width), bf16), result, x)
    for dx in (1, 3, 2):
        along_x = put(along_x, hop(result, dx=dx), (x - dx) % NX)
    hidden_grad = put(jnp.zeros((NC, NX, part, width), bf16), along_x, c)
    hidden_grad = put(hidden_grad, hop(along_x, dc=1), 1 - c)
    table_grad = lax.dynamic_update_slice(
        jnp.zeros((vocab_rows, half), bf16),
        (own_grad[:, start:early].astype(f32) + received.astype(f32)).astype(bf16),
        (0, start),
    )
    table_grad = lax.dynamic_update_slice(
        table_grad, (own_grad[:, :start].astype(f32) + first_grad.astype(f32)).astype(bf16), (0, 0)
    )
    table_grad = lax.dynamic_update_slice(
        table_grad, (own_grad[:, early:].astype(f32) + late.astype(f32)).astype(bf16), (0, early)
    )
    return (hidden_grad.reshape(tok_rows, width), table_grad, token_loss)


def solution(mesh):
    placed = (P(("pipe", "dp"), None), P(), P(("pipe", "dp")), P(("vocab", "dp"), None))
    return jax.shard_map(
        on_device,
        mesh=mesh,
        in_specs=placed,
        out_specs=(P(("pipe", "dp"), None), P(("vocab", "dp"), "pipe"), P(("pipe", "dp"))),
        check_vma=False,
    )
```

```python
import jax
import jax.numpy as jnp
from jax import lax
from jax.experimental import pallas as pl
from jax.experimental.pallas import tpu as pltpu
from jax.sharding import PartitionSpec as P

NORM_EPS = 1e-06
NX, NC, NZ, NY = 4, 2, 4, 2
DIGIT = 256


def hop(array, dx=0, dc=0, dz=0, dy=0):
    pairs = []
    for x in range(NX):
        for c in range(NC):
            for z in range(NZ):
                for y in range(NY):
                    here = ((x * NC + c) * NZ + z) * NY + y
                    there = (
                        ((x + dx) % NX * NC + (c + dc) % NC) * NZ + (z + dz) % NZ
                    ) * NY + (y + dy) % NY
                    pairs.append((here, there))
    return lax.ppermute(array, ("vocab", "dp"), pairs)


def put(buffer, block, *lead):
    block = block.reshape((1,) * len(lead) + buffer.shape[len(lead):])
    start = tuple(lead) + (0,) * (buffer.ndim - len(lead))
    return lax.dynamic_update_slice(buffer, block, start)


def take(buffer, *lead):
    start = tuple(lead) + (0,) * (buffer.ndim - len(lead))
    sizes = (1,) * len(lead) + buffer.shape[len(lead):]
    return lax.dynamic_slice(buffer, start, sizes).reshape(buffer.shape[len(lead):])


def dot(a, b, contract, out=jnp.float32):
    return lax.dot_general(
        a, b, (contract, ((), ())), preferred_element_type=jnp.float32
    ).astype(out)


def backward_kernel(place, hidden, gain, mine1, mine2, far, result):
    part, width = hidden.shape
    own = mine1[...]
    other = mine2[...] + far[...].astype(jnp.float32)
    first = place[1] == 0
    grad = jnp.concatenate(
        [jnp.where(first, own, other), jnp.where(first, other, own)], axis=1
    )
    wide = hidden[...].astype(jnp.float32)
    inverse = lax.rsqrt(jnp.mean(wide * wide, axis=1, keepdims=True) + NORM_EPS)
    upward = grad * gain[...].astype(jnp.float32)
    inner_sum = jnp.sum(upward * wide, axis=1, keepdims=True)
    result[...] = (
        inverse * upward - wide * (inverse * inverse * inverse) * inner_sum / width
    ).astype(jnp.bfloat16)


def backward_call(place, hidden, gain, mine1, mine2, far, part):
    width = hidden.shape[1]
    whole = lambda a: pl.BlockSpec(a.shape, lambda i, p: (0, 0))
    return pl.pallas_call(
        backward_kernel,
        grid_spec=pltpu.PrefetchScalarGridSpec(
            num_scalar_prefetch=1,
            grid=(1,),
            in_specs=[
                pl.BlockSpec((part, width), lambda i, p: (p[0], 0)),
                pl.BlockSpec((1, width), lambda i, p: (0, 0)),
                whole(mine1), whole(mine2), whole(far),
            ],
            out_specs=pl.BlockSpec((part, width), lambda i, p: (0, 0)),
        ),
        out_shape=jax.ShapeDtypeStruct((part, width), jnp.bfloat16),
        compiler_params=pltpu.CompilerParams(vmem_limit_bytes=32 << 20),
        name="backward",
    )(place, hidden, gain.reshape(1, width), mine1, mine2, far)


def on_device(hidden, gain, targets, table):
    tok_rows, width = hidden.shape
    vocab_rows = table.shape[0]
    half = width // 2
    bf16, f32 = jnp.bfloat16, jnp.float32
    vocab, dp, pipe = lax.axis_index("vocab"), lax.axis_index("dp"), lax.axis_index("pipe")
    x, c = vocab // NC, vocab % NC
    z, y = dp // NY, dp % NY
    group = NX * NC * NZ * NY
    part = tok_rows // (NX * NC)
    side = tok_rows // NC
    far = side * NZ * NY
    first = c * side + x * part
    own_col, other_col = pipe * half, (1 - pipe) * half

    gain_wide = gain.astype(f32)
    place = jnp.stack([c * NX + x, pipe]).astype(jnp.int32)

    def scale(rows):
        wide = rows.astype(f32)
        inverse = lax.rsqrt(jnp.mean(wide * wide, axis=1, keepdims=True) + NORM_EPS)
        return (wide * inverse * gain_wide).astype(bf16)

    normed_mine = scale(lax.dynamic_slice_in_dim(hidden, first, part))
    mine1 = lax.dynamic_slice(normed_mine, (0, own_col), (part, half))
    digits = jnp.stack([targets // DIGIT, targets % DIGIT]).astype(bf16)
    digits = jnp.pad(digits, ((0, part - 2), (0, 0)))
    seed = jnp.concatenate([mine1, digits], axis=1)
    seed = jnp.broadcast_to(seed[None], (NZ * NY, part, half + tok_rows))
    near = lax.all_to_all(seed, "dp", 0, 0, tiled=True)
    normed_side = scale(lax.dynamic_slice_in_dim(hidden, c * side, side))
    mine2 = lax.dynamic_slice(normed_side, (0, other_col), (side, half))
    mine2, near = lax.optimization_barrier((mine2, near))
    rows1 = lax.all_gather(near[:, :, :half].reshape(-1, half), "vocab", axis=0, tiled=True)

    partner = hop(mine2, dy=1)
    rows2 = jnp.zeros((NC, NY, NZ, side, half), bf16)
    own_rows = put(jnp.zeros((NZ, side, half), bf16), mine2, z)
    far_rows = put(jnp.zeros((NZ, side, half), bf16), partner, z)
    near1, near3, near2 = (hop(mine2, dz=dz) for dz in (1, 3, 2))
    far2, far1, far3 = hop(partner, dz=2), hop(near1, dy=1), hop(near3, dy=1)
    near2, far1 = lax.optimization_barrier((near2, far1))
    for dz, near_block, far_block in ((1, near1, far1), (3, near3, far3), (2, near2, far2)):
        own_rows = put(own_rows, near_block, (z - dz) % NZ)
        far_rows = put(far_rows, far_block, (z - dz) % NZ)
    for block, at in ((own_rows, y), (far_rows, 1 - y)):
        rows2 = put(rows2, block, c, at)
        rows2 = put(rows2, hop(block, dc=1), 1 - c, at)
    rows2 = rows2.reshape(-1, half)

    wanted = near[:, :2, half:].astype(jnp.int32)
    wanted = wanted[:, 0] * DIGIT + wanted[:, 1]
    wanted = wanted.reshape(NZ * NY, NC, NX, part).transpose(2, 1, 0, 3).reshape(-1)

    table1 = lax.dynamic_slice(table, (0, own_col), (vocab_rows, half))
    table2 = lax.dynamic_slice(table, (0, other_col), (vocab_rows, half))
    table1, table2, wanted = lax.optimization_barrier((table1, table2, wanted))
    logits1 = dot(rows1, table1, ((1,), (1,)))
    logits2 = dot(rows2, table2, ((1,), (1,)))
    logits2 = logits2.reshape(NC, NY, NZ, NX, part, vocab_rows).transpose(3, 0, 2, 1, 4, 5)
    logits2 = logits2.reshape(logits1.shape)
    logits1, logits2 = lax.optimization_barrier((logits1, logits2))
    logits = logits1 + logits2

    first_row = (vocab * NZ * NY + dp) * vocab_rows
    columns = lax.broadcasted_iota(jnp.int32, (1, vocab_rows), 1) + first_row
    is_target = columns == wanted[:, None]
    picked = jnp.sum(jnp.where(is_target, logits, jnp.zeros_like(logits)), axis=1)
    local_top = jnp.max(logits, axis=1)
    local_norm = local_top + jnp.log(jnp.sum(jnp.exp(logits - local_top[:, None]), axis=1))
    picked = picked.reshape(NX * NC, NZ * NY, part).transpose(1, 0, 2).reshape(NZ * NY, tok_rows)
    stats = jnp.concatenate(
        [
            jnp.broadcast_to(local_norm[None], (group, local_norm.shape[0])),
            jnp.tile(picked, (NX * NC, 1)),
        ],
        axis=1,
    )
    stats = lax.all_to_all(stats, ("vocab", "dp"), 0, 0, tiled=True)
    norms, picks = stats[:, : local_norm.shape[0]], stats[:, local_norm.shape[0] :]
    row_top = jnp.max(norms, axis=0)
    log_norm = row_top + jnp.log(jnp.sum(jnp.exp(norms - row_top), axis=0))
    own_norm = lax.dynamic_slice_in_dim(
        log_norm.reshape(NX * NC, NZ * NY, part), dp, 1, axis=1
    ).reshape(-1)
    token_loss = (own_norm - jnp.sum(picks, axis=0)).reshape(NX, NC, part)
    token_loss = token_loss.transpose(1, 0, 2).reshape(-1)

    grad_a = (jnp.exp(logits - log_norm[:, None]) - is_target.astype(f32)).astype(bf16)
    grad_b = grad_a.reshape(NX, NC, NZ, NY, part, vocab_rows).transpose(1, 3, 2, 0, 4, 5)
    grad_b = grad_b.reshape(NC, far, vocab_rows)

    sums1 = dot(grad_a, table1, ((1,), (0,)), bf16)
    sums1, grad_a, grad_b = lax.optimization_barrier((sums1, grad_a, grad_b))
    over_vocab = lax.psum_scatter(sums1, "vocab", scatter_dimension=0, tiled=True)
    sent = dot(take(grad_b, 1 - c), table2, ((1,), (0,)), bf16)
    start, early = half // 14, half * 11 // 14
    first_grad = dot(grad_b.reshape(-1, vocab_rows), rows2[:, :start], ((0,), (0,)), bf16)
    sent, first_grad, grad_b = lax.optimization_barrier((sent, first_grad, grad_b))
    swap = [(0, 1), (1, 0)]
    first_grad = lax.ppermute(first_grad, "pipe", swap)
    sent = hop(sent, dc=1)

    all_b = grad_b.reshape(-1, vocab_rows)
    sent_grad = dot(all_b, rows2[:, start:early], ((0,), (0,)), bf16)
    sent_grad, grad_b = lax.optimization_barrier((sent_grad, grad_b))
    received = lax.ppermute(sent_grad, "pipe", swap)
    first_grad, grad_b = lax.optimization_barrier((first_grad, grad_b))

    sums2 = (dot(take(grad_b, c), table2, ((1,), (0,))) + sent.astype(f32)).astype(bf16)
    sums2 = sums2.reshape(NY, NZ, side, half)
    z_blocks = [
        lax.dynamic_slice_in_dim(sums2, (z + dz) % NZ, 1, axis=1).reshape(NY, NX, part, half)
        for dz in range(NZ)
    ]
    *z_blocks, grad_a, grad_b = lax.optimization_barrier((*z_blocks, grad_a, grad_b))
    late_grad = dot(grad_b.reshape(-1, vocab_rows), rows2[:, early:], ((0,), (0,)), bf16)
    own_grad = dot(grad_a, rows1, ((0,), (0,)), bf16)

    total2 = z_blocks[0].astype(f32)
    for dz in (1, 3, 2):
        total2 = total2 + hop(z_blocks[dz], dz=dz).astype(f32)
    total2 = total2.astype(bf16)
    x_blocks = [
        lax.dynamic_slice_in_dim(total2, (x + dx) % NX, 1, axis=1).reshape(NY, part, half)
        for dx in range(NX)
    ]
    *x_blocks, own_grad, late_grad, over_vocab = lax.optimization_barrier(
        (*x_blocks, own_grad, late_grad, over_vocab)
    )
    mine2 = x_blocks[0].astype(f32)
    for dx in (1, 3, 2):
        mine2 = mine2 + hop(x_blocks[dx], dx=dx).astype(f32)
    mine2 = mine2.astype(bf16)
    blocks = lax.all_to_all(over_vocab.reshape(-1, part, half), "dp", 0, 0, tiled=True)
    mine1 = jnp.sum(blocks.astype(f32), axis=0)
    mine1, mine2, received = lax.optimization_barrier((mine1, mine2, received))
    far = hop(take(mine2, 1 - y), dy=1)
    mine2 = take(mine2, y).astype(f32)
    far, late, received = lax.optimization_barrier((far, late_grad, received))
    late = lax.ppermute(late, "pipe", swap)

    result = backward_call(place, hidden, gain, mine1, mine2, far, part)
    along_x = put(jnp.zeros((NX, part, width), bf16), result, x)
    for dx in (1, 3, 2):
        along_x = put(along_x, hop(result, dx=dx), (x - dx) % NX)
    hidden_grad = put(jnp.zeros((NC, NX, part, width), bf16), along_x, c)
    hidden_grad = put(hidden_grad, hop(along_x, dc=1), 1 - c)
    table_grad = lax.dynamic_update_slice(
        jnp.zeros((vocab_rows, half), bf16),
        (own_grad[:, start:early].astype(f32) + received.astype(f32)).astype(bf16),
        (0, start),
    )
    table_grad = lax.dynamic_update_slice(
        table_grad, (own_grad[:, :start].astype(f32) + first_grad.astype(f32)).astype(bf16), (0, 0)
    )
    table_grad = lax.dynamic_update_slice(
        table_grad, (own_grad[:, early:].astype(f32) + late.astype(f32)).astype(bf16), (0, early)
    )
    return (hidden_grad.reshape(tok_rows, width), table_grad, token_loss)


def solution(mesh):
    placed = (P(("pipe", "dp"), None), P(), P(("pipe", "dp")), P(("vocab", "dp"), None))
    return jax.shard_map(
        on_device,
        mesh=mesh,
        in_specs=placed,
        out_specs=(P(("pipe", "dp"), None), P(("vocab", "dp"), "pipe"), P(("pipe", "dp"))),
        check_vma=False,
    )
```
